256 devices in a mesh: ctx: 256 (over z, x, y, core).
Axes of the slice: x: 4, y: 4, z: 8, core: 2. Of those that a mesh axis runs over, the one named last changes fastest.
Arguments:
- projected: bfloat16 [3, 32768, 512], P(None, 'ctx'), may hold values from -6 to 6
- short_taps: float32 [3, 3, 512], replicated, may hold values from -3.5 to 3.5
- long_filter: float32 [32768, 512], P('ctx'), may hold values from -0.03125 to 0.03125
- skip_weight: float32 [512], replicated, may hold values from -4 to 4
Outputs:
- gated: bfloat16 [32768, 512], P('ctx')
The draws below stay inside these ranges and needn't reach their ends.
All inputs are finite; a program needn't handle non-finite values.
Results may differ from the reference program's by a relative error of at most 0.0012.
Values may be sent and summed in bfloat16 or wider, within the bound.
A program may use at most 64 MiB of HBM per device.

```python
import jax
import jax.numpy as jnp

CH = 512
SEQ = 32768


def levels(key, shape, split, low, high):
    def one(position, parts):
        steps = jax.random.uniform(jax.random.fold_in(jax.random.fold_in(key, 6), position), (parts,), jnp.float32, low / len(split), high / len(split))
        return jnp.repeat(jnp.exp(steps), shape[position] // parts).reshape((-1,) + (1,) * (len(shape) - position - 1))

    factor_of = one(*split[0])
    for cut in split[1:]:
        factor_of = factor_of * one(*cut)
    return factor_of


def gaussian(own_key, extent, deviation, limit, pieces=(), held_as=jnp.bfloat16):
    array = deviation * jax.random.normal(own_key, extent, jnp.float32)
    if pieces:
        array = array * levels(own_key, extent, pieces, -0.22, 0.18)
    return jnp.clip(array, -limit, limit).astype(held_as)


def setup_inputs(seed: int = 0) -> dict:
    streams_of = jax.random.split(jax.random.key(seed), 5)
    return {
        "projected": gaussian(streams_of[0], (3, SEQ, CH), 1.0, 6.0, ((1, 256),)),
        "short_taps": gaussian(streams_of[1], (3, 3, CH), 3 ** -0.5, 3.5, (), jnp.float32),
        "long_filter": gaussian(streams_of[2], (SEQ, CH), SEQ ** -0.5, 0.03125, ((0, 256),), jnp.float32),
        "skip_weight": gaussian(streams_of[3], (CH,), 1.0, 4.0, (), jnp.float32),
    }


def shifted(signal, lag_count):
    return jnp.pad(signal, ((0, 0), (lag_count, 0), (0, 0)))[:, :SEQ, :]


def reference(projected, short_taps, long_filter, skip_weight):
    signal = projected.astype(jnp.float32)
    shorted = (short_taps[:, 0, None, :] * signal
               + short_taps[:, 1, None, :] * shifted(signal, 1)
               + short_taps[:, 2, None, :] * shifted(signal, 2))
    mixed_in = shorted[1] * shorted[2]
    padded_len = 2 * SEQ
    spectrum = jnp.fft.rfft(mixed_in, n=padded_len, axis=0) * jnp.fft.rfft(long_filter, n=padded_len, axis=0)
    convolved = jnp.fft.irfft(spectrum, n=padded_len, axis=0)[:SEQ]
    return (shorted[0] * (convolved + skip_weight * mixed_in)).astype(jnp.bfloat16)
```

```python
import functools
import math

import jax
import jax.numpy as jnp
import ml_dtypes
import numpy as np
from jax import lax
from jax.experimental import pallas as pl
from jax.experimental.pallas import tpu as pltpu
from jax.sharding import PartitionSpec as P

MESH = pl.DeviceIdType.MESH
F32, BF16 = jnp.float32, jnp.bfloat16

DEPTH = 8
ROWS = 128
LANES = 128
PAIR = 2


def halves(table):
    high = table.astype(np.float32).astype(ml_dtypes.bfloat16)
    low = (table - high.astype(np.float64)).astype(ml_dtypes.bfloat16)
    return np.stack([high, low])


def tables(count):
    total = count * ROWS
    segment = np.arange(count)
    phase = 2 * np.pi * ((4 * segment[:, None] + 1) * segment[None, :] % (4 * count)) / (4 * count)
    outer = np.concatenate([np.cos(phase), -np.sin(phase)])
    inner_index = np.arange(ROWS)
    angle = 2 * np.pi * (inner_index[:, None] * inner_index[None, :] % ROWS) / ROWS
    cos, sin = np.cos(angle), np.sin(angle)
    inner = np.block([[cos, -sin], [sin, cos]])
    inner_back = np.block([[cos, sin], [-sin, cos]])
    turn = 2 * np.pi * ((4 * segment[:, None] + 1) * inner_index[None, :]) / (4 * total)
    twiddle = np.stack([np.cos(turn), -np.sin(turn)]).astype(np.float32)
    return halves(outer), halves(outer.T / total), halves(inner), halves(inner_back), twiddle


def split(value):
    high = value.astype(BF16)
    return high, (value - high.astype(F32)).astype(BF16)


def dot(a, b):
    return jnp.dot(a, b, preferred_element_type=F32)


def table_times(table, value):
    high, low = split(value)
    return dot(table[0], high) + (dot(table[0], low) + dot(table[1], high))


def times_table(value, table):
    high, low = split(value)
    return dot(high, table[0]) + (dot(high, table[1]) + dot(low, table[0]))


def spectrum(signal, outer, inner, twiddle):
    count = signal.shape[0]
    stage = table_times(outer, signal)
    parts = []
    for channel in range(PAIR):
        lanes = slice(channel * LANES, (channel + 1) * LANES)
        re, im = stage[:count, lanes], stage[count:, lanes]
        parts.append(
            jnp.concatenate([re * twiddle[0] - im * twiddle[1], re * twiddle[1] + im * twiddle[0]], axis=1)
        )
    return times_table(jnp.concatenate(parts, axis=0), inner)


def signal_of(product, outer_back, inner_back, twiddle):
    count = product.shape[0] // PAIR
    stage = times_table(product, inner_back)
    reals, imags = [], []
    for channel in range(PAIR):
        re = stage[channel * count : (channel + 1) * count, :LANES]
        im = stage[channel * count : (channel + 1) * count, LANES:]
        reals.append(re * twiddle[0] + im * twiddle[1])
        imags.append(im * twiddle[0] - re * twiddle[1])
    both = jnp.concatenate([jnp.concatenate(reals, axis=1), jnp.concatenate(imags, axis=1)], axis=0)
    return table_times(outer_back, both)


def kernel(
    count,
    projected,
    taps,
    long_filter,
    skip,
    outer_hbm,
    outer_back_hbm,
    inner_hbm,
    inner_back_hbm,
    twiddle_hbm,
    gated,
    streams,
    filt,
    outer,
    outer_back,
    inner,
    inner_back,
    twiddle,
    rim_out,
    rim_in,
    turned,
    h_out,
    h_z,
    h_mid,
    h_in,
    x_out,
    x_p,
    x_mid,
    x_in,
    y_out,
    y_z,
    y_mid,
    y_in,
    mixed,
    query,
    spec_h,
    load_sem,
    send_sem,
    recv_sem,
):
    me = lax.axis_index("ctx")
    plane = count // DEPTH
    z = me // plane
    p = me % plane
    right = (me + 1) % count
    left = (me + count - 1) % count

    def plane_peer(step):
        q = (p + step) % plane
        return q, z * plane + q

    def z_peer(step):
        q = (z + step) % DEPTH
        return q, q * plane + p

    loads = [
        pltpu.make_async_copy(src, dst, load_sem.at[i])
        for i, (src, dst) in enumerate(
            [
                (long_filter, filt),
                (projected, streams),
                (outer_hbm, outer),
                (inner_hbm, inner),
                (twiddle_hbm, twiddle),
                (inner_back_hbm, inner_back),
                (outer_back_hbm, outer_back),
            ]
        )
    ]
    for load in loads:
        load.start()

    barrier = pltpu.get_barrier_semaphore()

    def signal(device):
        pl.semaphore_signal(barrier, inc=1, device_id=(device,), device_id_type=MESH)

    @pl.loop(1, plane)
    def _(step):
        signal(plane_peer(step)[1])

    @pl.loop(1, DEPTH)
    def _(step):
        signal(z_peer(step)[1])

    signal(right)
    signal(left)

    def rows(index, size):
        return pl.ds(pl.multiple_of(index * size, size), size)

    def send(phase, src, dst, device):
        pltpu.make_async_remote_copy(
            src_ref=src,
            dst_ref=dst,
            send_sem=send_sem.at[phase],
            recv_sem=recv_sem.at[phase],
            device_id=(device,),
            device_id_type=MESH,
        ).start()

    def arrived(phase, src, dst, size):
        done = pltpu.make_async_remote_copy(
            src_ref=src.at[pl.ds(0, size)],
            dst_ref=dst.at[pl.ds(0, size)],
            send_sem=send_sem.at[phase],
            recv_sem=recv_sem.at[phase],
            device_id=(right,),
            device_id_type=MESH,
        )
        done.wait_send()
        done.wait_recv()

    def over_plane(phase, src, dst):
        size = 2 * DEPTH

        @pl.loop(1, plane)
        def _(step):
            q, device = plane_peer(step)
            send(phase, src.at[rows(q, size)], dst.at[rows(p, size)], device)

        dst[rows(p, size), :] = src[rows(p, size), :]

    def over_z(phase, src, dst):
        size = 2 * plane

        @pl.loop(1, DEPTH)
        def _(step):
            q, device = z_peer(step)
            send(phase, src.at[rows(q, size)], dst.at[rows(z, size)], device)

        dst[rows(z, size), :] = src[rows(z, size), :]

    plane_rows = 2 * DEPTH * (plane - 1)
    z_rows = 2 * plane * (DEPTH - 1)

    def by_z(src, dst):
        for index in range(2 * DEPTH):
            dst[pl.ds(index * plane, plane), :] = src[pl.ds(index, plane, 2 * DEPTH), :]

    loads[0].wait()
    for block in range(4):
        lanes = pl.ds(block * LANES, LANES)
        turned[lanes, :] = filt[:, lanes].T
    by_z(turned, h_out)

    loads[1].wait()
    for stream in range(3):
        tail = streams[stream, ROWS - 16 : ROWS, :].astype(F32)
        rim_out[2 * stream : 2 * stream + 2, :] = tail[14:16, :]
    rim_out[6:8, :] = jnp.zeros_like(rim_out[6:8, :])

    pl.semaphore_wait(barrier, plane - 1 + DEPTH - 1 + 2)
    send(0, rim_out, rim_in, right)
    over_z(1, h_out, h_z)
    arrived(0, rim_out, rim_in, 8)

    row = lax.broadcasted_iota(jnp.int32, (ROWS, 1), 0)
    first = me == 0

    def short(stream):
        here = streams[stream].astype(F32)
        rim = jnp.where(first, 0.0, rim_in[2 * stream : 2 * stream + 2, :])
        one = jnp.where(row == 0, rim[1:2, :], pltpu.roll(here, 1, 0))
        two = jnp.where(row == 0, rim[0:1, :], jnp.where(row == 1, rim[1:2, :], pltpu.roll(here, 2, 0)))
        return (
            taps[stream, 0:1, :] * here + taps[stream, 1:2, :] * one + taps[stream, 2:3, :] * two
        )

    mixed[...] = short(1) * short(2)
    for block in range(4):
        lanes = pl.ds(block * LANES, LANES)
        x_out[lanes, :] = mixed[:, lanes].T
    over_plane(2, x_out, x_p)

    arrived(1, h_out, h_z, z_rows)
    for q in range(plane):
        for channel in range(PAIR):
            h_mid[pl.ds(q * 2 * DEPTH + channel * DEPTH, DEPTH), :] = h_z[
                pl.ds(channel * plane + q, DEPTH, 2 * plane), :
            ]
    arrived(2, x_out, x_p, plane_rows)
    by_z(x_p, x_mid)
    over_z(4, x_mid, x_in)
    over_plane(3, h_mid, h_in)

    query[...] = short(0)
    mixed[...] = skip[...] * mixed[...]
    for load in loads[2:]:
        load.wait()

    arrived(3, h_mid, h_in, plane_rows)
    channels = []
    for channel in range(PAIR):
        channels.append(
            jnp.concatenate(
                [h_in[pl.ds(channel * DEPTH + s, plane, 2 * DEPTH), :] for s in range(DEPTH)], axis=0
            )
        )
    spec_h[...] = spectrum(jnp.concatenate(channels, axis=1), outer, inner, twiddle)

    arrived(4, x_mid, x_in, z_rows)
    channels = []
    for channel in range(PAIR):
        channels.append(
            jnp.concatenate(
                [x_in[pl.ds((2 * s + channel) * plane, plane), :] for s in range(DEPTH)], axis=0
            )
        )
    spec_x = spectrum(jnp.concatenate(channels, axis=1), outer, inner, twiddle)
    xr, xi = spec_x[:, :LANES], spec_x[:, LANES:]
    hr, hi = spec_h[:, :LANES], spec_h[:, LANES:]
    product = jnp.concatenate([xr * hr - xi * hi, xr * hi + xi * hr], axis=1)
    result = signal_of(product, outer_back, inner_back, twiddle)
    for s in range(DEPTH):
        for channel in range(PAIR):
            y_out[pl.ds((2 * s + channel) * plane, plane), :] = result[
                s * plane : (s + 1) * plane, channel * LANES : (channel + 1) * LANES
            ]
    over_z(5, y_out, y_z)
    arrived(5, y_out, y_z, z_rows)
    for q in range(plane):
        y_mid[pl.ds(q * 2 * DEPTH, 2 * DEPTH), :] = y_z[pl.ds(q, 2 * DEPTH, plane), :]
    over_plane(6, y_mid, y_in)
    arrived(6, y_mid, y_in, plane_rows)
    for block in range(4):
        lanes = pl.ds(block * LANES, LANES)
        convolved = y_in[lanes, :].T
        gated[:, lanes] = (query[:, lanes] * (convolved + mixed[:, lanes])).astype(BF16)


def per_device(count, consts, projected, short_taps, long_filter, skip_weight):
    channels = long_filter.shape[1]
    outer, outer_back, inner, inner_back, twiddle = consts
    block = pltpu.VMEM((channels, LANES), F32)
    wide = pltpu.VMEM((ROWS, channels), F32)
    vmem = pl.BlockSpec(memory_space=pltpu.VMEM)
    anywhere = pl.BlockSpec(memory_space=pl.ANY)
    return pl.pallas_call(
        functools.partial(kernel, count),
        out_shape=jax.ShapeDtypeStruct((ROWS, channels), BF16),
        in_specs=[anywhere, vmem, anywhere, vmem] + [anywhere] * 5,
        out_specs=vmem,
        scratch_shapes=[
            pltpu.VMEM(projected.shape, BF16),
            wide,
            *[pltpu.VMEM(c.shape, c.dtype) for c in consts],
            pltpu.VMEM((8, channels), F32),
            pltpu.VMEM((8, channels), F32),
            *[block] * 13,
            wide,
            wide,
            pltpu.VMEM((PAIR * count, 2 * LANES), F32),
            pltpu.SemaphoreType.DMA((7,)),
            pltpu.SemaphoreType.DMA((7,)),
            pltpu.SemaphoreType.DMA((7,)),
        ],
        compiler_params=pltpu.CompilerParams(
            collective_id=0, has_side_effects=True, vmem_limit_bytes=60 * 1024 * 1024
        ),
    )(projected, short_taps, long_filter, skip_weight.reshape(1, channels), *consts)


def solution(mesh):
    count = mesh.shape["ctx"]
    consts = [jnp.asarray(t) for t in tables(count)]
    return jax.shard_map(
        functools.partial(per_device, count, consts),
        mesh=mesh,
        in_specs=(P(None, "ctx", None), P(), P("ctx", None), P()),
        out_specs=P("ctx", None),
        check_vma=False,
    )
```

```python
import functools
import math

import jax
import jax.numpy as jnp
import ml_dtypes
import numpy as np
from jax import lax
from jax.experimental import pallas as pl
from jax.experimental.pallas import tpu as pltpu
from jax.sharding import PartitionSpec as P

MESH = pl.DeviceIdType.MESH
F32, BF16 = jnp.float32, jnp.bfloat16

DEPTH = 8
ROWS = 128
LANES = 128
PAIR = 2
GROUP = 8
BATCH = 15
STRIDE = 37


def halves(table):
    high = table.astype(np.float32).astype(ml_dtypes.bfloat16)
    low = (table - high.astype(np.float64)).astype(ml_dtypes.bfloat16)
    return np.stack([high, low])


def tables(count):
    total = count * ROWS
    segment = np.arange(count)
    phase = 2 * np.pi * ((4 * segment[:, None] + 1) * segment[None, :] % (4 * count)) / (4 * count)
    outer = np.concatenate([np.cos(phase), -np.sin(phase)])
    inner_index = np.arange(ROWS)
    angle = 2 * np.pi * (inner_index[:, None] * inner_index[None, :] % ROWS) / ROWS
    cos, sin = np.cos(angle), np.sin(angle)
    inner = np.block([[cos, -sin], [sin, cos]])
    inner_back = np.block([[cos, sin], [-sin, cos]])
    turn = 2 * np.pi * ((4 * segment[:, None] + 1) * inner_index[None, :]) / (4 * total)
    twiddle = np.stack([np.cos(turn), -np.sin(turn)]).astype(np.float32)
    return halves(outer), halves(outer.T / total), halves(inner), halves(inner_back), twiddle


def split(value):
    high = value.astype(BF16)
    return high, (value - high.astype(F32)).astype(BF16)


def dot(a, b):
    return jnp.dot(a, b, preferred_element_type=F32)


def table_times(table, value):
    high, low = split(value)
    return dot(table[0], high) + (dot(table[0], low) + dot(table[1], high))


def times_table(value, table):
    high, low = split(value)
    return dot(high, table[0]) + (dot(high, table[1]) + dot(low, table[0]))


def spectrum(signal, outer, inner, twiddle):
    count = signal.shape[0]
    stage = table_times(outer, signal)
    parts = []
    for channel in range(PAIR):
        lanes = slice(channel * LANES, (channel + 1) * LANES)
        re, im = stage[:count, lanes], stage[count:, lanes]
        parts.append(
            jnp.concatenate([re * twiddle[0] - im * twiddle[1], re * twiddle[1] + im * twiddle[0]], axis=1)
        )
    return times_table(jnp.concatenate(parts, axis=0), inner)


def signal_of(product, outer_back, inner_back, twiddle):
    count = product.shape[0] // PAIR
    stage = times_table(product, inner_back)
    reals, imags = [], []
    for channel in range(PAIR):
        re = stage[channel * count : (channel + 1) * count, :LANES]
        im = stage[channel * count : (channel + 1) * count, LANES:]
        reals.append(re * twiddle[0] + im * twiddle[1])
        imags.append(im * twiddle[0] - re * twiddle[1])
    both = jnp.concatenate([jnp.concatenate(reals, axis=1), jnp.concatenate(imags, axis=1)], axis=0)
    return table_times(outer_back, both)


def kernel(
    count,
    projected,
    taps,
    long_filter,
    skip,
    outer_hbm,
    outer_back_hbm,
    inner_hbm,
    inner_back_hbm,
    twiddle_hbm,
    gated,
    streams,
    filt,
    outer,
    outer_back,
    inner,
    inner_back,
    twiddle,
    rim_out,
    rim_in,
    h_out,
    h_z,
    h_mid,
    h_in,
    x_out,
    x_in,
    y_out,
    y_in,
    mixed,
    query,
    spec_h,
    load_sem,
    send_sem,
    recv_sem,
    ready,
):
    me = lax.axis_index("ctx")
    plane = count // DEPTH
    z = me // plane
    p = me % plane
    unit = me % GROUP
    right = (me + 1) % count
    left = (me + count - 1) % count

    loads = [
        pltpu.make_async_copy(src, dst, load_sem.at[i])
        for i, (src, dst) in enumerate(
            [
                (long_filter, filt),
                (projected, streams),
                (outer_hbm, outer),
                (inner_hbm, inner),
                (twiddle_hbm, twiddle),
                (inner_back_hbm, inner_back),
                (outer_back_hbm, outer_back),
            ]
        )
    ]
    loads[0].start()

    barrier = pltpu.get_barrier_semaphore()

    def signal(semaphore, device):
        pl.semaphore_signal(semaphore, inc=1, device_id=(device,), device_id_type=MESH)

    def over_group(semaphore):
        for step in range(1, GROUP):
            signal(semaphore, me - unit + lax.rem(unit + step, GROUP))

    def over_plane(semaphore):
        for step in range(1, plane // GROUP):
            signal(semaphore, z * plane + lax.rem(p + step * GROUP, plane))

    def over_z(semaphore):
        for step in range(1, DEPTH):
            signal(semaphore, lax.rem(me + step * plane, count))

    over_z(barrier)
    signal(barrier, right)
    signal(barrier, left)
    over_plane(barrier)
    over_group(barrier)
    for load in loads[1:]:
        load.start()

    def copy(phase, src, dst, device):
        return pltpu.make_async_remote_copy(
            src_ref=src,
            dst_ref=dst,
            send_sem=send_sem.at[phase],
            recv_sem=recv_sem.at[phase],
            device_id=(device,),
            device_id_type=MESH,
        )

    def own_rows(device):
        return pl.ds(pl.multiple_of(device * PAIR, PAIR), PAIR)

    def exchange(phase, src, dst):
        @pl.loop(0, (count - 1) // BATCH)
        def _(batch):
            for step in range(1, BATCH + 1):
                device = lax.rem(me + (batch * BATCH + step) * STRIDE, count)
                copy(phase, src.at[own_rows(device)], dst.at[own_rows(me)], device).start()

        dst[own_rows(me), :] = src[own_rows(me), :]

    def arrived(phase, src, dst, own):
        rows = pl.ds(0, PAIR * count - own)
        done = copy(phase, src.at[rows], dst.at[rows], right)
        done.wait_send()
        done.wait_recv()

    loads[0].wait()
    for block in range(4):
        lanes = pl.ds(block * LANES, LANES)
        h_out[lanes, :] = filt[:, lanes].T

    loads[1].wait()
    for stream in range(3):
        tail = streams[stream, ROWS - 16 : ROWS, :].astype(F32)
        rim_out[2 * stream : 2 * stream + 2, :] = tail[14:16, :]
    rim_out[6:8, :] = jnp.zeros_like(rim_out[6:8, :])

    pl.semaphore_wait(barrier, GROUP - 1 + plane // GROUP - 1 + DEPTH - 1 + 2)
    over_plane(ready.at[0])
    rim = copy(0, rim_out, rim_in, right)
    rim.start()
    column = PAIR * plane

    def piece(index, size):
        return pl.ds(pl.multiple_of(index * size, size), size)

    for step in range(1, DEPTH):
        other = lax.rem(z + step, DEPTH)
        copy(1, h_out.at[piece(other, column)], h_z.at[piece(z, column)], other * plane + p).start()
    h_z[piece(z, column), :] = h_out[piece(z, column), :]

    pl.semaphore_wait(ready.at[0], plane // GROUP - 1)
    over_z(ready.at[1])
    rim.wait()

    row = lax.broadcasted_iota(jnp.int32, (ROWS, 1), 0)
    first = me == 0

    def short(stream):
        here = streams[stream].astype(F32)
        rim = jnp.where(first, 0.0, rim_in[2 * stream : 2 * stream + 2, :])
        one = jnp.where(row == 0, rim[1:2, :], pltpu.roll(here, 1, 0))
        two = jnp.where(row == 0, rim[0:1, :], jnp.where(row == 1, rim[1:2, :], pltpu.roll(here, 2, 0)))
        return (
            taps[stream, 0:1, :] * here + taps[stream, 1:2, :] * one + taps[stream, 2:3, :] * two
        )

    mixed[...] = short(1) * short(2)
    for block in range(4):
        lanes = pl.ds(block * LANES, LANES)
        x_out[lanes, :] = mixed[:, lanes].T
    pl.semaphore_wait(ready.at[1], DEPTH - 1)
    exchange(2, x_out, x_in)

    arrived(1, h_out, h_z, column)
    part = PAIR * DEPTH
    for other in range(plane):
        for c in range(PAIR):
            h_mid[pl.ds(other * part + c * DEPTH, DEPTH), :] = h_z[pl.ds(PAIR * other + c, DEPTH, column), :]

    @pl.loop(1, plane)
    def _(step):
        other = lax.rem(p + step, plane)
        copy(4, h_mid.at[piece(other, part)], h_in.at[piece(p, part)], z * plane + other).start()

    h_in[piece(p, part), :] = h_mid[piece(p, part), :]

    query[...] = short(0)
    mixed[...] = skip[...] * mixed[...]
    for load in loads[2:]:
        load.wait()

    arrived(4, h_mid, h_in, part)
    filters = [
        jnp.concatenate([h_in[pl.ds(c * DEPTH + s, plane, part), :] for s in range(DEPTH)], axis=0)
        for c in range(PAIR)
    ]
    spec_h[...] = spectrum(jnp.concatenate(filters, axis=1), outer, inner, twiddle)

    arrived(2, x_out, x_in, PAIR)
    signals = [x_in[pl.ds(c, count, PAIR), :] for c in range(PAIR)]
    spec_x = spectrum(jnp.concatenate(signals, axis=1), outer, inner, twiddle)
    xr, xi = spec_x[:, :LANES], spec_x[:, LANES:]
    hr, hi = spec_h[:, :LANES], spec_h[:, LANES:]
    product = jnp.concatenate([xr * hr - xi * hi, xr * hi + xi * hr], axis=1)
    result = signal_of(product, outer_back, inner_back, twiddle)
    for c in range(PAIR):
        y_out[pl.ds(c, count, PAIR), :] = result[:, c * LANES : (c + 1) * LANES]
    exchange(3, y_out, y_in)
    arrived(3, y_out, y_in, PAIR)
    for block in range(4):
        lanes = pl.ds(block * LANES, LANES)
        convolved = y_in[lanes, :].T
        gated[:, lanes] = (query[:, lanes] * (convolved + mixed[:, lanes])).astype(BF16)


def per_device(count, consts, projected, short_taps, long_filter, skip_weight):
    channels = long_filter.shape[1]
    outer, outer_back, inner, inner_back, twiddle = consts
    block = pltpu.VMEM((channels, LANES), F32)
    wide = pltpu.VMEM((ROWS, channels), F32)
    vmem = pl.BlockSpec(memory_space=pltpu.VMEM)
    anywhere = pl.BlockSpec(memory_space=pl.ANY)
    return pl.pallas_call(
        functools.partial(kernel, count),
        out_shape=jax.ShapeDtypeStruct((ROWS, channels), BF16),
        in_specs=[anywhere, vmem, anywhere, vmem] + [anywhere] * 5,
        out_specs=vmem,
        scratch_shapes=[
            pltpu.VMEM(projected.shape, BF16),
            wide,
            *[pltpu.VMEM(c.shape, c.dtype) for c in consts],
            pltpu.VMEM((8, channels), F32),
            pltpu.VMEM((8, channels), F32),
            *[block] * 8,
            wide,
            wide,
            pltpu.VMEM((PAIR * count, 2 * LANES), F32),
            pltpu.SemaphoreType.DMA((7,)),
            pltpu.SemaphoreType.DMA((5,)),
            pltpu.SemaphoreType.DMA((5,)),
            pltpu.SemaphoreType.REGULAR((2,)),
        ],
        compiler_params=pltpu.CompilerParams(
            collective_id=0, has_side_effects=True, vmem_limit_bytes=60 * 1024 * 1024
        ),
    )(projected, short_taps, long_filter, skip_weight.reshape(1, channels), *consts)


def solution(mesh):
    count = mesh.shape["ctx"]
    consts = [jnp.asarray(t) for t in tables(count)]
    return jax.shard_map(
        functools.partial(per_device, count, consts),
        mesh=mesh,
        in_specs=(P(None, "ctx", None), P(), P("ctx", None), P()),
        out_specs=P("ctx", None),
        check_vma=False,
    )
```

```python
import functools
import math

import jax
import jax.numpy as jnp
import ml_dtypes
import numpy as np
from jax import lax
from jax.experimental import pallas as pl
from jax.experimental.pallas import tpu as pltpu
from jax.sharding import PartitionSpec as P

MESH = pl.DeviceIdType.MESH
F32, BF16 = jnp.float32, jnp.bfloat16

DEPTH = 8
ROWS = 128
LANES = 128
CODE_SCALE = 1.5 * 2.0**20
PAIR = 2
GROUP = 8
BATCH = 8


def halves(table):
    high = table.astype(np.float32).astype(ml_dtypes.bfloat16)
    low = (table - high.astype(np.float64)).astype(ml_dtypes.bfloat16)
    return np.stack([high, low])


def tables(count):
    total = count * ROWS
    segment = np.arange(count)
    phase = 2 * np.pi * ((4 * segment[:, None] + 1) * segment[None, :] % (4 * count)) / (4 * count)
    outer = np.concatenate([np.cos(phase), -np.sin(phase)])
    inner_index = np.arange(ROWS)
    angle = 2 * np.pi * (inner_index[:, None] * inner_index[None, :] % ROWS) / ROWS
    cos, sin = np.cos(angle), np.sin(angle)
    inner = np.block([[cos, -sin], [sin, cos]])
    inner_back = np.block([[cos, sin], [-sin, cos]])
    turn = 2 * np.pi * ((4 * segment[:, None] + 1) * inner_index[None, :]) / (4 * total)
    twiddle = np.stack([np.cos(turn), -np.sin(turn)]).astype(np.float32)
    return halves(outer), halves(outer.T / total), halves(inner), halves(inner_back), twiddle


def split(value):
    high = value.astype(BF16)
    return high, (value - high.astype(F32)).astype(BF16)


def dot(a, b):
    return jnp.dot(a, b, preferred_element_type=F32)


def table_times(table, value):
    high, low = split(value)
    return dot(table[0], high) + (dot(table[0], low) + dot(table[1], high))


def times_table(value, table):
    high, low = split(value)
    return dot(high, table[0]) + (dot(high, table[1]) + dot(low, table[0]))


def spectrum(signal, outer, inner, twiddle):
    count = signal.shape[0]
    stage = table_times(outer, signal)
    parts = []
    for channel in range(PAIR):
        lanes = slice(channel * LANES, (channel + 1) * LANES)
        re, im = stage[:count, lanes], stage[count:, lanes]
        parts.append(
            jnp.concatenate([re * twiddle[0] - im * twiddle[1], re * twiddle[1] + im * twiddle[0]], axis=1)
        )
    return times_table(jnp.concatenate(parts, axis=0), inner)


def signal_of(product, outer_back, inner_back, twiddle):
    count = product.shape[0] // PAIR
    stage = times_table(product, inner_back)
    reals, imags = [], []
    for channel in range(PAIR):
        re = stage[channel * count : (channel + 1) * count, :LANES]
        im = stage[channel * count : (channel + 1) * count, LANES:]
        reals.append(re * twiddle[0] + im * twiddle[1])
        imags.append(im * twiddle[0] - re * twiddle[1])
    both = jnp.concatenate([jnp.concatenate(reals, axis=1), jnp.concatenate(imags, axis=1)], axis=0)
    return table_times(outer_back, both)


def coded(value):
    power = value * CODE_SCALE
    for _ in range(3):
        power = power * power
    return jnp.where(value < 0, -power, power).astype(BF16)


def decoded(code):
    power = code.astype(F32)
    size = jnp.abs(power)
    for _ in range(3):
        size = jnp.sqrt(size)
    return jnp.where(power < 0, -size, size) * (1.0 / CODE_SCALE)


def kernel(
    count,
    projected,
    taps,
    long_filter,
    skip,
    outer_hbm,
    outer_back_hbm,
    inner_hbm,
    inner_back_hbm,
    twiddle_hbm,
    gated,
    streams,
    filt,
    outer,
    outer_back,
    inner,
    inner_back,
    twiddle,
    rim_out,
    rim_in,
    h_out,
    h_z,
    h_mid,
    h_in,
    h_wide,
    x_out,
    x_in,
    y_out,
    y_in,
    mixed,
    query,
    spec_h,
    load_sem,
    send_sem,
    recv_sem,
    ready,
):
    me = lax.axis_index("ctx")
    plane = count // DEPTH
    z = me // plane
    p = me % plane
    unit = me % GROUP
    right = (me + 1) % count
    left = (me + count - 1) % count

    loads = [
        pltpu.make_async_copy(src, dst, load_sem.at[i])
        for i, (src, dst) in enumerate(
            [
                (long_filter, filt),
                (projected, streams),
                (outer_hbm, outer),
                (inner_hbm, inner),
                (twiddle_hbm, twiddle),
                (inner_back_hbm, inner_back),
                (outer_back_hbm, outer_back),
            ]
        )
    ]
    loads[0].start()

    barrier = pltpu.get_barrier_semaphore()

    def signal(semaphore, device):
        pl.semaphore_signal(semaphore, inc=1, device_id=(device,), device_id_type=MESH)

    def over_group(semaphore):
        for step in range(1, GROUP):
            signal(semaphore, me - unit + lax.rem(unit + step, GROUP))

    def over_plane(semaphore):
        for step in range(1, plane // GROUP):
            signal(semaphore, z * plane + lax.rem(p + step * GROUP, plane))

    def over_z(semaphore):
        for step in range(1, DEPTH):
            signal(semaphore, lax.rem(me + step * plane, count))

    over_z(barrier)
    signal(barrier, right)
    signal(barrier, left)
    over_plane(barrier)
    over_group(barrier)
    for load in loads[1:]:
        load.start()

    def copy(phase, src, dst, device):
        return pltpu.make_async_remote_copy(
            src_ref=src,
            dst_ref=dst,
            send_sem=send_sem.at[phase],
            recv_sem=recv_sem.at[phase],
            device_id=(device,),
            device_id_type=MESH,
        )

    def own_rows(device):
        return pl.ds(pl.multiple_of(device * PAIR, PAIR), PAIR)

    def exchange(phase, src, dst):
        def to(far, near):
            device = lax.rem(z + far, DEPTH) * plane + lax.rem(p + near, plane)
            copy(phase, src.at[own_rows(device)], dst.at[own_rows(me)], device).start()

        half = DEPTH // 2
        batches = plane // BATCH

        @pl.loop(0, batches)
        def _(batch):
            for step in range(BATCH):
                to(half, plane // 2 + batch * BATCH + step)

        @pl.loop(0, (half - 1) * batches)
        def _(batch):
            off = 1 + batch // batches
            for step in range(BATCH):
                near = plane // 2 + batch % batches * BATCH + step
                to(half - off, near)
                to(half + off, near)

        @pl.loop(1, plane)
        def _(step):
            to(0, step)

        dst[own_rows(me), :] = src[own_rows(me), :]

    def arrived(phase, src, dst, own):
        rows = pl.ds(0, PAIR * count - own)
        done = copy(phase, src.at[rows], dst.at[rows], right)
        done.wait_send()
        done.wait_recv()

    loads[0].wait()
    for block in range(4):
        lanes = pl.ds(block * LANES, LANES)
        h_out[lanes, :] = coded(filt[:, lanes].T)

    loads[1].wait()
    for stream in range(3):
        tail = streams[stream, ROWS - 16 : ROWS, :].astype(F32)
        rim_out[2 * stream : 2 * stream + 2, :] = tail[14:16, :]
    rim_out[6:8, :] = jnp.zeros_like(rim_out[6:8, :])

    pl.semaphore_wait(barrier, GROUP - 1 + plane // GROUP - 1 + DEPTH - 1 + 2)
    over_z(ready.at[0])
    rim = copy(0, rim_out, rim_in, right)
    rim.start()
    column = PAIR * plane

    def piece(index, size):
        return pl.ds(pl.multiple_of(index * size, size), size)

    for step in (4, 3, 5, 2, 6, 1, 7):
        other = lax.rem(z + step, DEPTH)
        copy(1, h_out.at[piece(other, column)], h_z.at[piece(z, column)], other * plane + p).start()
    h_z[piece(z, column), :] = h_out[piece(z, column), :]

    pl.semaphore_wait(ready.at[0], DEPTH - 1)
    over_plane(ready.at[1])
    rim.wait()

    row = lax.broadcasted_iota(jnp.int32, (ROWS, 1), 0)
    first = me == 0

    def short(stream):
        here = streams[stream].astype(F32)
        rim = jnp.where(first, 0.0, rim_in[2 * stream : 2 * stream + 2, :])
        one = jnp.where(row == 0, rim[1:2, :], pltpu.roll(here, 1, 0))
        two = jnp.where(row == 0, rim[0:1, :], jnp.where(row == 1, rim[1:2, :], pltpu.roll(here, 2, 0)))
        return (
            taps[stream, 0:1, :] * here + taps[stream, 1:2, :] * one + taps[stream, 2:3, :] * two
        )

    mixed[...] = short(1) * short(2)
    for block in range(4):
        lanes = pl.ds(block * LANES, LANES)
        x_out[lanes, :] = mixed[:, lanes].T
    pl.semaphore_wait(ready.at[1], plane // GROUP - 1)
    exchange(2, x_out, x_in)

    arrived(1, h_out, h_z, column)
    part = PAIR * DEPTH
    h_wide[...] = h_z[...].astype(F32)
    for other in range(plane):
        rows = [h_wide[pl.ds(PAIR * other + c, DEPTH, column), :] for c in range(PAIR)]
        h_mid[pl.ds(other * part, part), :] = jnp.concatenate(rows, axis=0).astype(BF16)

    @pl.loop(1, plane)
    def _(step):
        other = lax.rem(p + step, plane)
        copy(4, h_mid.at[piece(other, part)], h_in.at[piece(p, part)], z * plane + other).start()

    h_in[piece(p, part), :] = h_mid[piece(p, part), :]

    query[...] = short(0)
    mixed[...] = skip[...] * mixed[...]
    for load in loads[2:]:
        load.wait()

    arrived(4, h_mid, h_in, part)
    h_wide[...] = decoded(h_in[...])
    filters = [
        jnp.concatenate([h_wide[pl.ds(c * DEPTH + s, plane, part), :] for s in range(DEPTH)], axis=0)
        for c in range(PAIR)
    ]
    spec_h[...] = spectrum(jnp.concatenate(filters, axis=1), outer, inner, twiddle)

    arrived(2, x_out, x_in, PAIR)
    signals = [x_in[pl.ds(c, count, PAIR), :] for c in range(PAIR)]
    spec_x = spectrum(jnp.concatenate(signals, axis=1), outer, inner, twiddle)
    xr, xi = spec_x[:, :LANES], spec_x[:, LANES:]
    hr, hi = spec_h[:, :LANES], spec_h[:, LANES:]
    product = jnp.concatenate([xr * hr - xi * hi, xr * hi + xi * hr], axis=1)
    result = signal_of(product, outer_back, inner_back, twiddle)
    for c in range(PAIR):
        y_out[pl.ds(c, count, PAIR), :] = result[:, c * LANES : (c + 1) * LANES]
    exchange(3, y_out, y_in)
    arrived(3, y_out, y_in, PAIR)
    for block in range(4):
        lanes = pl.ds(block * LANES, LANES)
        convolved = y_in[lanes, :].T
        gated[:, lanes] = (query[:, lanes] * (convolved + mixed[:, lanes])).astype(BF16)


def per_device(count, consts, projected, short_taps, long_filter, skip_weight):
    channels = long_filter.shape[1]
    outer, outer_back, inner, inner_back, twiddle = consts
    block = pltpu.VMEM((channels, LANES), F32)
    code = pltpu.VMEM((channels, LANES), BF16)
    wide = pltpu.VMEM((ROWS, channels), F32)
    vmem = pl.BlockSpec(memory_space=pltpu.VMEM)
    anywhere = pl.BlockSpec(memory_space=pl.ANY)
    return pl.pallas_call(
        functools.partial(kernel, count),
        out_shape=pltpu.VMEM((ROWS, channels), BF16),
        in_specs=[anywhere, vmem, anywhere, vmem] + [anywhere] * 5,
        out_specs=vmem,
        scratch_shapes=[
            pltpu.VMEM(projected.shape, BF16),
            wide,
            *[pltpu.VMEM(c.shape, c.dtype) for c in consts],
            pltpu.VMEM((8, channels), F32),
            pltpu.VMEM((8, channels), F32),
            *[code] * 4,
            *[block] * 5,
            wide,
            wide,
            pltpu.VMEM((PAIR * count, 2 * LANES), F32),
            pltpu.SemaphoreType.DMA((7,)),
            pltpu.SemaphoreType.DMA((5,)),
            pltpu.SemaphoreType.DMA((5,)),
            pltpu.SemaphoreType.REGULAR((2,)),
        ],
        compiler_params=pltpu.CompilerParams(
            collective_id=0, has_side_effects=True, vmem_limit_bytes=60 * 1024 * 1024
        ),
    )(projected, short_taps, long_filter, skip_weight.reshape(1, channels), *consts)


def solution(mesh):
    count = mesh.shape["ctx"]
    consts = [jnp.asarray(t) for t in tables(count)]
    return jax.shard_map(
        functools.partial(per_device, count, consts),
        mesh=mesh,
        in_specs=(P(None, "ctx", None), P(), P("ctx", None), P()),
        out_specs=P("ctx", None),
        check_vma=False,
    )
```

```python
import functools
import math

import jax
import jax.numpy as jnp
import ml_dtypes
import numpy as np
from jax import lax
from jax.experimental import pallas as pl
from jax.experimental.pallas import tpu as pltpu
from jax.sharding import PartitionSpec as P

MESH = pl.DeviceIdType.MESH
F32, BF16 = jnp.float32, jnp.bfloat16

DEPTH = 8
ROWS = 128
LANES = 128
CODE_LIMIT = 1.4 * 2.0**15
CODE_SCALE = 1.5 * 2.0**20
PAIR = 2
BATCH = 8


def halves(table):
    high = table.astype(np.float32).astype(ml_dtypes.bfloat16)
    low = (table - high.astype(np.float64)).astype(ml_dtypes.bfloat16)
    return np.stack([high, low])


def tables(count):
    total = count * ROWS
    segment = np.arange(count)
    phase = 2 * np.pi * ((4 * segment[:, None] + 1) * segment[None, :] % (4 * count)) / (4 * count)
    outer = np.concatenate([np.cos(phase), -np.sin(phase)])
    inner_index = np.arange(ROWS)
    angle = 2 * np.pi * (inner_index[:, None] * inner_index[None, :] % ROWS) / ROWS
    cos, sin = np.cos(angle), np.sin(angle)
    inner = np.block([[cos, -sin], [sin, cos]])
    inner_back = np.block([[cos, sin], [-sin, cos]])
    turn = 2 * np.pi * ((4 * segment[:, None] + 1) * inner_index[None, :]) / (4 * total)
    twiddle = np.stack([np.cos(turn), -np.sin(turn)]).astype(np.float32)
    return halves(outer), halves(outer.T / total), halves(inner), halves(inner_back), twiddle


def split(value):
    high = value.astype(BF16)
    return high, (value - high.astype(F32)).astype(BF16)


def dot(a, b):
    return jnp.dot(a, b, preferred_element_type=F32)


def table_times(table, value):
    high, low = split(value)
    return dot(table[0], high) + (dot(table[0], low) + dot(table[1], high))


def times_table(value, table):
    high, low = split(value)
    return dot(high, table[0]) + (dot(high, table[1]) + dot(low, table[0]))


def spectrum(signal, outer, inner, twiddle):
    count = signal.shape[0]
    stage = table_times(outer, signal)
    parts = []
    for channel in range(PAIR):
        lanes = slice(channel * LANES, (channel + 1) * LANES)
        re, im = stage[:count, lanes], stage[count:, lanes]
        parts.append(
            jnp.concatenate([re * twiddle[0] - im * twiddle[1], re * twiddle[1] + im * twiddle[0]], axis=1)
        )
    return times_table(jnp.concatenate(parts, axis=0), inner)


def signal_of(product, outer_back, inner_back, twiddle):
    count = product.shape[0] // PAIR
    stage = times_table(product, inner_back)
    reals, imags = [], []
    for channel in range(PAIR):
        re = stage[channel * count : (channel + 1) * count, :LANES]
        im = stage[channel * count : (channel + 1) * count, LANES:]
        reals.append(re * twiddle[0] + im * twiddle[1])
        imags.append(im * twiddle[0] - re * twiddle[1])
    both = jnp.concatenate([jnp.concatenate(reals, axis=1), jnp.concatenate(imags, axis=1)], axis=0)
    return table_times(outer_back, both)


def coded(value):
    power = value
    for _ in range(3):
        power = power * power
    return jnp.where(value < 0, -power, power).astype(BF16)


def decoded(code):
    power = code.astype(F32)
    size = jnp.abs(power)
    for _ in range(3):
        size = jnp.sqrt(size)
    return jnp.where(power < 0, -size, size)


def kernel(
    count,
    projected,
    taps,
    long_filter,
    skip,
    outer_hbm,
    outer_back_hbm,
    inner_hbm,
    inner_back_hbm,
    twiddle_hbm,
    gated,
    streams,
    filt,
    outer,
    outer_back,
    inner,
    inner_back,
    twiddle,
    rim_out,
    rim_in,
    h_out,
    h_z,
    h_mid,
    h_in,
    h_wide,
    x_out,
    x_in,
    size_out,
    size_z,
    size_in,
    y_wide,
    y_out,
    y_in,
    mixed,
    query,
    spec_h,
    load_sem,
    send_sem,
    recv_sem,
    ready,
):
    me = lax.axis_index("ctx")
    plane = count // DEPTH
    z = me // plane
    p = me % plane
    right = (me + 1) % count
    left = (me + count - 1) % count

    loads = [
        pltpu.make_async_copy(src, dst, load_sem.at[i])
        for i, (src, dst) in enumerate(
            [
                (long_filter, filt),
                (projected, streams),
                (outer_hbm, outer),
                (inner_hbm, inner),
                (twiddle_hbm, twiddle),
                (inner_back_hbm, inner_back),
                (outer_back_hbm, outer_back),
            ]
        )
    ]
    loads[0].start()

    barrier = pltpu.get_barrier_semaphore()

    def signal(semaphore, device):
        pl.semaphore_signal(semaphore, inc=1, device_id=(device,), device_id_type=MESH)

    def over_z(semaphore):
        for step in range(1, DEPTH):
            signal(semaphore, lax.rem(me + step * plane, count))

    over_z(barrier)
    signal(barrier, right)
    signal(barrier, left)
    for step in range(1, plane):
        signal(barrier, z * plane + lax.rem(p + step, plane))
    for load in loads[1:]:
        load.start()

    def copy(phase, src, dst, device):
        return pltpu.make_async_remote_copy(
            src_ref=src,
            dst_ref=dst,
            send_sem=send_sem.at[phase],
            recv_sem=recv_sem.at[phase],
            device_id=(device,),
            device_id_type=MESH,
        )

    def own_rows(device):
        return pl.ds(pl.multiple_of(device * PAIR, PAIR), PAIR)

    def exchange(phase, src, dst, between=None):
        def to(far, near):
            device = lax.rem(z + far, DEPTH) * plane + lax.rem(p + near, plane)
            copy(phase, src.at[own_rows(device)], dst.at[own_rows(me)], device).start()

        half = DEPTH // 2
        batches = plane // BATCH

        @pl.loop(0, batches)
        def _(batch):
            for step in range(BATCH):
                to(half, plane // 2 + batch * BATCH + step)

        def around(batch):
            off = 1 + batch // batches
            for step in range(BATCH):
                near = plane // 2 + batch % batches * BATCH + step
                to(half - off, near)
                to(half + off, near)

        pl.loop(0, batches)(around)
        if between is not None:
            between()
        pl.loop(batches, (half - 1) * batches)(around)

        @pl.loop(1, plane)
        def _(step):
            to(0, step)

        own = pltpu.make_async_copy(src.at[own_rows(me)], dst.at[own_rows(me)], load_sem.at[7])
        own.start()
        own.wait()

    def arrived(phase, src, dst, own):
        rows = pl.ds(0, dst.shape[0] - own)
        done = copy(phase, src.at[rows], dst.at[rows], right)
        done.wait_send()
        done.wait_recv()

    loads[0].wait()
    for block in range(4):
        lanes = pl.ds(block * LANES, LANES)
        h_out[lanes, :] = coded(filt[:, lanes].T * CODE_SCALE)

    loads[1].wait()
    for stream in range(3):
        tail = streams[stream, ROWS - 16 : ROWS, :].astype(F32)
        rim_out[2 * stream : 2 * stream + 2, :] = tail[14:16, :]
    rim_out[6:8, :] = jnp.zeros_like(rim_out[6:8, :])

    pl.semaphore_wait(barrier, plane - 1 + DEPTH - 1 + 2)
    over_z(ready)
    rim = copy(0, rim_out, rim_in, right)
    rim.start()
    column = PAIR * plane

    def piece(index, size):
        return pl.ds(pl.multiple_of(index * size, size), size)

    for step in (4, 3, 5, 2, 6, 1, 7):
        other = lax.rem(z + step, DEPTH)
        copy(1, h_out.at[piece(other, column)], h_z.at[piece(z, column)], other * plane + p).start()
    h_z[piece(z, column), :] = h_out[piece(z, column), :]

    rim.wait()

    row = lax.broadcasted_iota(jnp.int32, (ROWS, 1), 0)
    first = me == 0

    def short(stream):
        here = streams[stream].astype(F32)
        rim = jnp.where(first, 0.0, rim_in[2 * stream : 2 * stream + 2, :])
        one = jnp.where(row == 0, rim[1:2, :], pltpu.roll(here, 1, 0))
        two = jnp.where(row == 0, rim[0:1, :], jnp.where(row == 1, rim[1:2, :], pltpu.roll(here, 2, 0)))
        return (
            taps[stream, 0:1, :] * here + taps[stream, 1:2, :] * one + taps[stream, 2:3, :] * two
        )

    mixed[...] = short(1) * short(2)

    def energy(ref):
        return jnp.sum(ref[...] * ref[...], axis=(0, 1), keepdims=True)

    lane = lax.broadcasted_iota(jnp.int32, size_out.shape, 1)
    size_out[...] = jnp.where(lane < LANES // 2, energy(mixed), energy(filt))
    for step in range(1, DEPTH):
        to = lax.rem(z + step, DEPTH) * plane + p
        copy(5, size_out.at[pl.ds(0, 1)], size_z.at[pl.ds(z, 1)], to).start()
    size_z[pl.ds(z, 1), :] = size_out[0:1, :]
    for block in range(4):
        lanes = pl.ds(block * LANES, LANES)
        x_out[lanes, :] = mixed[:, lanes].T
    pl.semaphore_wait(ready, DEPTH - 1)
    part = PAIR * DEPTH

    def filter_in_plane():
        arrived(1, h_out, h_z, column)
        h_wide[...] = h_z[...].astype(F32)
        for other in range(plane):
            rows = [h_wide[pl.ds(PAIR * other + c, DEPTH, column), :] for c in range(PAIR)]
            h_mid[pl.ds(other * part, part), :] = jnp.concatenate(rows, axis=0).astype(BF16)

        @pl.loop(1, plane)
        def _(step):
            other = lax.rem(p + step, plane)
            copy(4, h_mid.at[piece(other, part)], h_in.at[piece(p, part)], z * plane + other).start()

        h_in[piece(p, part), :] = h_mid[piece(p, part), :]

    exchange(2, x_out, x_in, filter_in_plane)

    arrived(5, size_z, size_z, 1)

    @pl.loop(1, plane)
    def _(step):
        device = z * plane + lax.rem(p + step, plane)
        copy(6, size_z, size_in.at[piece(p, DEPTH)], device).start()

    size_in[piece(p, DEPTH), :] = size_z[...]

    query[...] = short(0)
    mixed[...] = skip[...] * mixed[...]
    for load in loads[2:]:
        load.wait()

    arrived(4, h_mid, h_in, part)
    h_wide[...] = decoded(h_in[...]) * (1.0 / CODE_SCALE)
    filters = [
        jnp.concatenate([h_wide[pl.ds(c * DEPTH + s, plane, part), :] for s in range(DEPTH)], axis=0)
        for c in range(PAIR)
    ]
    spec_h[...] = spectrum(jnp.concatenate(filters, axis=1), outer, inner, twiddle)

    arrived(2, x_out, x_in, PAIR)
    signals = [x_in[pl.ds(c, count, PAIR), :] for c in range(PAIR)]
    spec_x = spectrum(jnp.concatenate(signals, axis=1), outer, inner, twiddle)
    xr, xi = spec_x[:, :LANES], spec_x[:, LANES:]
    hr, hi = spec_h[:, :LANES], spec_h[:, LANES:]
    product = jnp.concatenate([xr * hr - xi * hi, xr * hi + xi * hr], axis=1)
    result = signal_of(product, outer_back, inner_back, twiddle)
    for c in range(PAIR):
        y_wide[pl.ds(c, count, PAIR), :] = result[:, c * LANES : (c + 1) * LANES]
    arrived(6, size_in, size_in, DEPTH)
    total = jnp.sum(size_in[...], axis=0, keepdims=True)
    reach = jnp.maximum(jnp.sqrt(total[:, :1]) * jnp.sqrt(total[:, LANES // 2 : LANES // 2 + 1]), 1e-12)
    y_out[...] = coded(y_wide[...] * (CODE_LIMIT / reach))
    exchange(3, y_out, y_in)
    arrived(3, y_out, y_in, PAIR)
    for block in range(4):
        lanes = pl.ds(block * LANES, LANES)
        convolved = (decoded(y_in[lanes, :]) * (reach * (1.0 / CODE_LIMIT))).T
        gated[:, lanes] = (query[:, lanes] * (convolved + mixed[:, lanes])).astype(BF16)


def per_device(count, consts, projected, short_taps, long_filter, skip_weight):
    channels = long_filter.shape[1]
    outer, outer_back, inner, inner_back, twiddle = consts
    block = pltpu.VMEM((channels, LANES), F32)
    code = pltpu.VMEM((channels, LANES), BF16)
    wide = pltpu.VMEM((ROWS, channels), F32)
    vmem = pl.BlockSpec(memory_space=pltpu.VMEM)
    anywhere = pl.BlockSpec(memory_space=pl.ANY)
    return pl.pallas_call(
        functools.partial(kernel, count),
        out_shape=pltpu.VMEM((ROWS, channels), BF16),
        in_specs=[anywhere, vmem, anywhere, vmem] + [anywhere] * 5,
        out_specs=vmem,
        scratch_shapes=[
            pltpu.VMEM(projected.shape, BF16),
            wide,
            *[pltpu.VMEM(c.shape, c.dtype) for c in consts],
            pltpu.VMEM((8, channels), F32),
            pltpu.VMEM((8, channels), F32),
            *[code] * 4,
            *[block] * 3,
            pltpu.VMEM((8, LANES), F32),
            pltpu.VMEM((DEPTH, LANES), F32),
            pltpu.VMEM((count, LANES), F32),
            block,
            *[code] * 2,
            wide,
            wide,
            pltpu.VMEM((PAIR * count, 2 * LANES), F32),
            pltpu.SemaphoreType.DMA((8,)),
            pltpu.SemaphoreType.DMA((7,)),
            pltpu.SemaphoreType.DMA((7,)),
            pltpu.SemaphoreType.REGULAR,
        ],
        compiler_params=pltpu.CompilerParams(
            collective_id=0, has_side_effects=True, vmem_limit_bytes=60 * 1024 * 1024
        ),
    )(projected, short_taps, long_filter, skip_weight.reshape(1, channels), *consts)


def solution(mesh):
    count = mesh.shape["ctx"]
    consts = [jnp.asarray(t) for t in tables(count)]
    return jax.shard_map(
        functools.partial(per_device, count, consts),
        mesh=mesh,
        in_specs=(P(None, "ctx", None), P(), P("ctx", None), P()),
        out_specs=P("ctx", None),
        check_vma=False,
    )
```

```python
import functools
import math

import jax
import jax.numpy as jnp
import ml_dtypes
import numpy as np
from jax import lax
from jax.experimental import pallas as pl
from jax.experimental.pallas import tpu as pltpu
from jax.sharding import PartitionSpec as P

MESH = pl.DeviceIdType.MESH
F32, BF16 = jnp.float32, jnp.bfloat16

DEPTH = 8
ROWS = 128
LANES = 128
CODE_LIMIT = 1.4 * 2.0**15
CODE_SCALE = 1.5 * 2.0**20
PAIR = 2
BATCH = 8


def halves(table):
    high = table.astype(np.float32).astype(ml_dtypes.bfloat16)
    low = (table - high.astype(np.float64)).astype(ml_dtypes.bfloat16)
    return np.stack([high, low])


def tables(count):
    total = count * ROWS
    segment = np.arange(count)
    phase = 2 * np.pi * ((4 * segment[:, None] + 1) * segment[None, :] % (4 * count)) / (4 * count)
    outer = np.concatenate([np.cos(phase), -np.sin(phase)])
    inner_index = np.arange(ROWS)
    angle = 2 * np.pi * (inner_index[:, None] * inner_index[None, :] % ROWS) / ROWS
    cos, sin = np.cos(angle), np.sin(angle)
    inner = np.block([[cos, -sin], [sin, cos]])
    inner_back = np.block([[cos, sin], [-sin, cos]])
    turn = 2 * np.pi * ((4 * segment[:, None] + 1) * inner_index[None, :]) / (4 * total)
    twiddle = np.stack([np.cos(turn), -np.sin(turn)]).astype(np.float32)
    return halves(outer), halves(outer.T / total), halves(inner), halves(inner_back), twiddle


def split(value):
    high = value.astype(BF16)
    return high, (value - high.astype(F32)).astype(BF16)


def dot(a, b):
    return jnp.dot(a, b, preferred_element_type=F32)


def table_times(table, value):
    high, low = split(value)
    return dot(table[0], high) + (dot(table[0], low) + dot(table[1], high))


def times_table(value, table):
    high, low = split(value)
    return dot(high, table[0]) + (dot(high, table[1]) + dot(low, table[0]))


def spectrum(signal, outer, inner, twiddle):
    count = signal.shape[0]
    stage = table_times(outer, signal)
    parts = []
    for channel in range(PAIR):
        lanes = slice(channel * LANES, (channel + 1) * LANES)
        re, im = stage[:count, lanes], stage[count:, lanes]
        parts.append(
            jnp.concatenate([re * twiddle[0] - im * twiddle[1], re * twiddle[1] + im * twiddle[0]], axis=1)
        )
    return times_table(jnp.concatenate(parts, axis=0), inner)


def signal_of(product, outer_back, inner_back, twiddle):
    count = product.shape[0] // PAIR
    stage = times_table(product, inner_back)
    reals, imags = [], []
    for channel in range(PAIR):
        re = stage[channel * count : (channel + 1) * count, :LANES]
        im = stage[channel * count : (channel + 1) * count, LANES:]
        reals.append(re * twiddle[0] + im * twiddle[1])
        imags.append(im * twiddle[0] - re * twiddle[1])
    both = jnp.concatenate([jnp.concatenate(reals, axis=1), jnp.concatenate(imags, axis=1)], axis=0)
    return table_times(outer_back, both)


def coded(value):
    power = value
    for _ in range(3):
        power = power * power
    return jnp.where(value < 0, -power, power).astype(BF16)


def decoded(code):
    power = code.astype(F32)
    size = jnp.abs(power)
    for _ in range(3):
        size = jnp.sqrt(size)
    return jnp.where(power < 0, -size, size)


def kernel(
    count,
    projected,
    taps,
    long_filter,
    skip,
    outer_hbm,
    outer_back_hbm,
    inner_hbm,
    inner_back_hbm,
    twiddle_hbm,
    gated,
    streams,
    filt,
    outer,
    outer_back,
    inner,
    inner_back,
    twiddle,
    rim_out,
    rim_in,
    h_out,
    h_z,
    h_mid,
    h_in,
    h_wide,
    x_out,
    x_in,
    size_out,
    size_z,
    size_in,
    y_wide,
    y_out,
    y_in,
    mixed,
    query,
    spec_h,
    load_sem,
    send_sem,
    recv_sem,
    ready,
):
    me = lax.axis_index("ctx")
    plane = count // DEPTH
    z = me // plane
    p = me % plane
    right = (me + 1) % count
    left = (me + count - 1) % count

    loads = [
        pltpu.make_async_copy(src, dst, load_sem.at[i])
        for i, (src, dst) in enumerate(
            [
                (long_filter, filt),
                (projected, streams),
                (outer_hbm, outer),
                (inner_hbm, inner),
                (twiddle_hbm, twiddle),
                (inner_back_hbm, inner_back),
                (outer_back_hbm, outer_back),
            ]
        )
    ]
    loads[0].start()

    barrier = pltpu.get_barrier_semaphore()

    def signal(semaphore, device):
        pl.semaphore_signal(semaphore, inc=1, device_id=(device,), device_id_type=MESH)

    def over_z(semaphore):
        for step in range(1, DEPTH):
            signal(semaphore, lax.rem(me + step * plane, count))

    over_z(barrier)
    signal(barrier, right)
    signal(barrier, left)
    for step in range(1, plane):
        signal(barrier, z * plane + lax.rem(p + step, plane))
    for load in loads[1:]:
        load.start()

    def copy(phase, src, dst, device):
        return pltpu.make_async_remote_copy(
            src_ref=src,
            dst_ref=dst,
            send_sem=send_sem.at[phase],
            recv_sem=recv_sem.at[phase],
            device_id=(device,),
            device_id_type=MESH,
        )

    def own_rows(device):
        return pl.ds(pl.multiple_of(device * PAIR, PAIR), PAIR)

    def exchange(phase, src, dst, between=None):
        def to(far, near):
            device = lax.rem(z + far, DEPTH) * plane + lax.rem(p + near, plane)
            copy(phase, src.at[own_rows(device)], dst.at[own_rows(me)], device).start()

        half = DEPTH // 2
        batches = plane // BATCH

        @pl.loop(0, batches)
        def _(batch):
            for step in range(BATCH):
                to(half, plane // 2 + batch * BATCH + step)

        def around(batch):
            off = 1 + batch // batches
            for step in range(BATCH):
                near = plane // 2 + batch % batches * BATCH + step
                to(half - off, near)
                to(half + off, near)

        pl.loop(0, (half - 1) * batches)(around)
        if between is not None:
            between()

        @pl.loop(1, plane)
        def _(step):
            to(0, step)

        own = pltpu.make_async_copy(src.at[own_rows(me)], dst.at[own_rows(me)], load_sem.at[7])
        own.start()
        own.wait()

    def arrived(phase, src, dst, own):
        rows = pl.ds(0, dst.shape[0] - own)
        done = copy(phase, src.at[rows], dst.at[rows], right)
        done.wait_send()
        done.wait_recv()

    loads[0].wait()
    for block in range(4):
        lanes = pl.ds(block * LANES, LANES)
        h_out[lanes, :] = coded(filt[:, lanes].T * CODE_SCALE)

    loads[1].wait()
    for stream in range(3):
        tail = streams[stream, ROWS - 16 : ROWS, :].astype(F32)
        rim_out[2 * stream : 2 * stream + 2, :] = tail[14:16, :]
    rim_out[6:8, :] = jnp.zeros_like(rim_out[6:8, :])

    pl.semaphore_wait(barrier, plane - 1 + DEPTH - 1 + 2)
    over_z(ready)
    rim = copy(0, rim_out, rim_in, right)
    rim.start()
    column = PAIR * plane

    def piece(index, size):
        return pl.ds(pl.multiple_of(index * size, size), size)

    for step in (4, 3, 5, 2, 6, 1, 7):
        other = lax.rem(z + step, DEPTH)
        copy(1, h_out.at[piece(other, column)], h_z.at[piece(z, column)], other * plane + p).start()
    h_z[piece(z, column), :] = h_out[piece(z, column), :]

    rim.wait()

    row = lax.broadcasted_iota(jnp.int32, (ROWS, 1), 0)
    first = me == 0

    def short(stream):
        here = streams[stream].astype(F32)
        rim = jnp.where(first, 0.0, rim_in[2 * stream : 2 * stream + 2, :])
        one = jnp.where(row == 0, rim[1:2, :], pltpu.roll(here, 1, 0))
        two = jnp.where(row == 0, rim[0:1, :], jnp.where(row == 1, rim[1:2, :], pltpu.roll(here, 2, 0)))
        return (
            taps[stream, 0:1, :] * here + taps[stream, 1:2, :] * one + taps[stream, 2:3, :] * two
        )

    mixed[...] = short(1) * short(2)

    def energy(ref):
        return jnp.sum(ref[...] * ref[...], axis=(0, 1), keepdims=True)

    lane = lax.broadcasted_iota(jnp.int32, size_out.shape, 1)
    size_out[...] = jnp.where(lane < LANES // 2, energy(mixed), energy(filt))
    for step in range(1, DEPTH):
        to = lax.rem(z + step, DEPTH) * plane + p
        copy(5, size_out.at[pl.ds(0, 1)], size_z.at[pl.ds(z, 1)], to).start()
    size_z[pl.ds(z, 1), :] = size_out[0:1, :]
    for block in range(4):
        lanes = pl.ds(block * LANES, LANES)
        x_out[lanes, :] = mixed[:, lanes].T
    pl.semaphore_wait(ready, DEPTH - 1)
    part = PAIR * DEPTH

    def filter_in_plane():
        arrived(1, h_out, h_z, column)
        h_wide[...] = h_z[...].astype(F32)
        for other in range(plane):
            rows = [h_wide[pl.ds(PAIR * other + c, DEPTH, column), :] for c in range(PAIR)]
            h_mid[pl.ds(other * part, part), :] = jnp.concatenate(rows, axis=0).astype(BF16)

        @pl.loop(1, plane)
        def _(step):
            other = lax.rem(p + step, plane)
            copy(4, h_mid.at[piece(other, part)], h_in.at[piece(p, part)], z * plane + other).start()

        h_in[piece(p, part), :] = h_mid[piece(p, part), :]

    exchange(2, x_out, x_in, filter_in_plane)

    arrived(5, size_z, size_z, 1)

    @pl.loop(1, plane)
    def _(step):
        device = z * plane + lax.rem(p + step, plane)
        copy(6, size_z, size_in.at[piece(p, DEPTH)], device).start()

    size_in[piece(p, DEPTH), :] = size_z[...]

    query[...] = short(0)
    mixed[...] = skip[...] * mixed[...]
    for load in loads[2:]:
        load.wait()

    arrived(4, h_mid, h_in, part)
    h_wide[...] = decoded(h_in[...]) * (1.0 / CODE_SCALE)
    filters = [
        jnp.concatenate([h_wide[pl.ds(c * DEPTH + s, plane, part), :] for s in range(DEPTH)], axis=0)
        for c in range(PAIR)
    ]
    spec_h[...] = spectrum(jnp.concatenate(filters, axis=1), outer, inner, twiddle)

    arrived(2, x_out, x_in, PAIR)
    signals = [x_in[pl.ds(c, count, PAIR), :] for c in range(PAIR)]
    spec_x = spectrum(jnp.concatenate(signals, axis=1), outer, inner, twiddle)
    xr, xi = spec_x[:, :LANES], spec_x[:, LANES:]
    hr, hi = spec_h[:, :LANES], spec_h[:, LANES:]
    product = jnp.concatenate([xr * hr - xi * hi, xr * hi + xi * hr], axis=1)
    result = signal_of(product, outer_back, inner_back, twiddle)
    for c in range(PAIR):
        y_wide[pl.ds(c, count, PAIR), :] = result[:, c * LANES : (c + 1) * LANES]
    arrived(6, size_in, size_in, DEPTH)
    total = jnp.sum(size_in[...], axis=0, keepdims=True)
    reach = jnp.maximum(jnp.sqrt(total[:, :1]) * jnp.sqrt(total[:, LANES // 2 : LANES // 2 + 1]), 1e-12)
    y_out[...] = coded(y_wide[...] * (CODE_LIMIT / reach))
    exchange(3, y_out, y_in)
    arrived(3, y_out, y_in, PAIR)
    for block in range(4):
        lanes = pl.ds(block * LANES, LANES)
        convolved = (decoded(y_in[lanes, :]) * (reach * (1.0 / CODE_LIMIT))).T
        gated[:, lanes] = (query[:, lanes] * (convolved + mixed[:, lanes])).astype(BF16)


def per_device(count, consts, projected, short_taps, long_filter, skip_weight):
    channels = long_filter.shape[1]
    outer, outer_back, inner, inner_back, twiddle = consts
    block = pltpu.VMEM((channels, LANES), F32)
    code = pltpu.VMEM((channels, LANES), BF16)
    wide = pltpu.VMEM((ROWS, channels), F32)
    vmem = pl.BlockSpec(memory_space=pltpu.VMEM)
    anywhere = pl.BlockSpec(memory_space=pl.ANY)
    return pl.pallas_call(
        functools.partial(kernel, count),
        out_shape=pltpu.VMEM((ROWS, channels), BF16),
        in_specs=[anywhere, vmem, anywhere, vmem] + [anywhere] * 5,
        out_specs=vmem,
        scratch_shapes=[
            pltpu.VMEM(projected.shape, BF16),
            wide,
            *[pltpu.VMEM(c.shape, c.dtype) for c in consts],
            pltpu.VMEM((8, channels), F32),
            pltpu.VMEM((8, channels), F32),
            *[code] * 4,
            *[block] * 3,
            pltpu.VMEM((8, LANES), F32),
            pltpu.VMEM((DEPTH, LANES), F32),
            pltpu.VMEM((count, LANES), F32),
            block,
            *[code] * 2,
            wide,
            wide,
            pltpu.VMEM((PAIR * count, 2 * LANES), F32),
            pltpu.SemaphoreType.DMA((8,)),
            pltpu.SemaphoreType.DMA((7,)),
            pltpu.SemaphoreType.DMA((7,)),
            pltpu.SemaphoreType.REGULAR,
        ],
        compiler_params=pltpu.CompilerParams(
            collective_id=0, has_side_effects=True, vmem_limit_bytes=60 * 1024 * 1024
        ),
    )(projected, short_taps, long_filter, skip_weight.reshape(1, channels), *consts)


def solution(mesh):
    count = mesh.shape["ctx"]
    consts = [jnp.asarray(t) for t in tables(count)]
    return jax.shard_map(
        functools.partial(per_device, count, consts),
        mesh=mesh,
        in_specs=(P(None, "ctx", None), P(), P("ctx", None), P()),
        out_specs=P("ctx", None),
        check_vma=False,
    )
```
